32 devices in a mesh: groups: 1, local: 32 (over z, y, x, core).
Axes of the slice: x: 2, y: 2, z: 4, core: 2. Of those that a mesh axis runs over, the one named last changes fastest.
Arguments:
- tokens: bfloat16 [2048, 2048], P(('groups', 'local')), may hold values from -6 to 6
- expert_ids: int32 [2048, 2], P(('groups', 'local')), may hold values from 0 to 3, all different within a row; in each aligned block of 64 rows (0 to 63, 64 to 127, ...) at most 48 rows name the same one
- gate_weights: float32 [2048, 2], P(('groups', 'local')), may hold values from 0.2 to 1
- norm_gain: float32 [2048], replicated, may hold values from 0.25 to 1.75
- norm_bias: float32 [2048], replicated, may hold values from -3 to 3
- w_in: bfloat16 [32, 2048, 1024], P('local'), may hold values from -0.125 to 0.125
- b_in: float32 [32, 1024], P('local'), may hold values from -4 to 4
- w_out: bfloat16 [32, 1024, 2048], P('local'), may hold values from -0.0625 to 0.0625
- b_out: float32 [4, 2048], replicated, may hold values from -3 to 3
Outputs:
- mixed_out: bfloat16 [2048, 2048], P(('groups', 'local'))
The draws below stay inside these ranges and needn't reach their ends.
Inputs may be any that keep to these rules, and one draw needn't show every extreme that they name: `expert_ids`: among the 64 tokens of one device, no expert is named by more than 48 pairs, a bound that some block reaches; a token's 2 experts differ.
All inputs are finite; a program needn't handle non-finite values.
Results may differ from the reference program's by a relative error of at most 0.008.
Values may be sent and summed in bfloat16 or wider, within the bound.
No kernel may reach another device: no remote copies, remote signals or barrier semaphores. Data moves between devices by JAX's collectives and lax.ppermute only.
A program may use at most 128 MiB of HBM per device.

```python
import math
import jax
import jax.numpy as jnp
import numpy as np
from jax import lax

D = 2048
HID = 8192
HID_DEV = 1024
TOP = 2
TOK_DEV = 64
SPLIT = 8
EXPERTS = 4
TOKENS = 2048
CAP = 48
N_LOCAL = 32


def level_of(stream_key, extent, pieces, least, high):
    loudness, own = 1.0, jax.random.fold_in(stream_key, 6)
    for position, parts in pieces:
        steps = jnp.exp(jax.random.uniform(jax.random.fold_in(own, position), (parts,), jnp.float32, least / len(pieces), high / len(pieces)))
        loudness = loudness * jnp.repeat(steps, extent[position] // parts).reshape([-1 if axis == position else 1 for axis in range(len(extent))])
    return loudness


def deal_out(own_key, own, number, rows, count, top, bound, skew):
    ranking = jax.random.permutation(own_key, count)
    crowded, common = portions_of(count, rows * top, bound, skew, True), portions_of(count, rows * top, bound, skew, False)
    places = jnp.arange(count)

    def named(tallies, offset_by):
        used = int((tallies > 0).sum())
        fixed = max(1, used // 4)
        passed = fixed + (places - fixed + offset_by * (used - fixed)) % max(1, count - fixed)
        return jnp.zeros((count,), jnp.int32).at[ranking[jnp.where(places < fixed, places, passed)]].set(jnp.asarray(tallies, jnp.int32))

    tallies = jnp.where(number % 4 == 0, named(crowded, number // 4), named(common, number - number // 4 - 1))
    mixed = jax.random.permutation(jax.random.fold_in(own, 3), count)
    donor, sink = mixed[0:count // 2 * 2:2], mixed[1:count // 2 * 2:2]
    margin = jnp.minimum(tallies[donor] - 1, bound - tallies[sink]) // 2
    margin = jnp.where((donor == ranking[0]) | (sink == ranking[0]) | (tallies[sink] == 0), 0, jnp.maximum(margin, 0))
    passed = jax.random.randint(jax.random.fold_in(own, 4), (count // 2,), 0, 1 << 20) % (margin + 1)
    tallies = tallies.at[donor].add(-passed).at[sink].add(passed)
    members = jnp.searchsorted(jnp.cumsum(tallies), jnp.arange(rows * top), side="right").astype(jnp.int32)
    table = members.reshape(top, rows).T
    table = table[jax.random.permutation(jax.random.fold_in(own, 1), rows)]
    offset_by = jax.random.randint(jax.random.fold_in(own, 2), (rows, 1), 0, top)
    return jnp.take_along_axis(table, (jnp.arange(top)[None, :] + offset_by) % top, axis=1)


def portions_of(count, total, most, lean, full):
    portions = [(1 << 20) // math.isqrt(grade ** lean) + 1 for grade in range(1, count + 1)]
    largest = most if full else min(most, max(-(-total // count), total * portions[0] // sum(portions)))
    least = 1 if total - largest >= count - 1 else 0
    given, rest = [largest] + [least] * (count - 1), total - largest - least * (count - 1)
    while rest > 0:
        candidates = [i for i in range(1, count) if given[i] < largest] or [i for i in range(1, count) if given[i] < most]
        mass, remaining = sum([portions[i] for i in candidates]), rest
        for i in candidates:
            addition = min(most - given[i], max(1, remaining * portions[i] // mass), rest)
            given[i] = given[i] + addition
            rest = rest - addition
    return np.array(given)


def bell_draw(rng, dims, scale, most, split=(), kind=jnp.bfloat16):
    level = level_of(rng, dims, split, -0.22, 0.18) if split else 1.0
    entries = jax.random.normal(rng, dims, jnp.float32) * scale * level
    return jnp.minimum(jnp.maximum(entries, -most), most).astype(kind)


def setup_inputs(seed: int = 0, part: int = 0) -> dict:
    seeds = jax.random.split(jax.random.key(seed), 10)
    part_keys = jax.random.split(jax.random.fold_in(seeds[9], part), 10)
    tokens = bell_draw(part_keys[0], (TOKENS, D), 1.0, 6.0, ((0, 32),))
    expert_ids_keys = jax.random.split(jax.random.fold_in(part_keys[1], 1), TOKENS // TOK_DEV)
    expert_ids_turns = jax.random.permutation(jax.random.fold_in(part_keys[1], 3), TOKENS // TOK_DEV)
    expert_ids = jax.vmap(lambda own, number: deal_out(jax.random.fold_in(part_keys[1], 2), own, number, TOK_DEV, EXPERTS, TOP, CAP, 2))(expert_ids_keys, expert_ids_turns).reshape((TOKENS, TOP))
    gate_weights = jnp.clip(0.2 + 0.8 * jax.random.uniform(part_keys[2], (TOKENS, TOP), jnp.float32) ** level_of(part_keys[2], (TOKENS, TOP), ((0, 32),), -0.2, 0.2), 0.2, 1.0)
    norm_gain = jnp.clip(1.0 + 0.15 * jax.random.normal(seeds[3], (D,), jnp.float32), 0.25, 1.75)
    norm_bias = bell_draw(seeds[4], (D,), 0.5, 3.0, (), jnp.float32)
    w_in = bell_draw(seeds[5], (EXPERTS * SPLIT, D, HID_DEV), D ** -0.5, 0.125, ((0, 32),))
    b_in = bell_draw(seeds[6], (EXPERTS * SPLIT, HID_DEV), 1.0, 4.0, ((0, 32),), jnp.float32)
    w_out = bell_draw(seeds[7], (EXPERTS * SPLIT, HID_DEV, D), HID ** -0.5, 0.0625, ((0, 32),))
    b_out = bell_draw(seeds[8], (EXPERTS, D), 0.5, 3.0, (), jnp.float32)
    return {"tokens": tokens, "expert_ids": expert_ids, "gate_weights": gate_weights, "norm_gain": norm_gain, "norm_bias": norm_bias, "w_in": w_in, "b_in": b_in, "w_out": w_out, "b_out": b_out}


def layer_norm(values, gain, bias):
    floats = values.astype(jnp.float32)
    row_mean = lax.optimization_barrier(jnp.mean(floats, axis=-1, keepdims=True))
    centered = floats - row_mean
    row_var = lax.optimization_barrier(jnp.mean(centered * centered, axis=-1, keepdims=True))
    return centered * lax.rsqrt(row_var + 1e-05) * gain + bias

def one_expert(operands):
    row_block, weight_in, bias_in, weight_out, bias_out = operands
    hidden = jnp.einsum('rd,sdh->srh', row_block.astype(jnp.float32), weight_in.astype(jnp.float32)) + bias_in[:, None, :]
    hidden = jnp.maximum(hidden, 0.0).astype(jnp.bfloat16)
    partial_value = jnp.einsum('srh,shd->srd', hidden.astype(jnp.float32), weight_out.astype(jnp.float32))
    partial_value = partial_value.astype(jnp.bfloat16).astype(jnp.float32)
    return lax.optimization_barrier(jnp.sum(partial_value, axis=0)) + bias_out[None, :]

def reference(tokens, expert_ids, gate_weights, norm_gain, norm_bias, w_in, b_in, w_out, b_out):
    normed = layer_norm(tokens, norm_gain, norm_bias).astype(jnp.bfloat16)
    flat_ids = expert_ids.reshape(N_LOCAL, TOK_DEV * TOP)
    onehot = (flat_ids[:, :, None] == jnp.arange(EXPERTS, dtype=jnp.int32)[None, None, :]).astype(jnp.int32)
    slot_rank = lax.optimization_barrier(jnp.sum(jnp.cumsum(onehot, axis=1) * onehot, axis=2)) - 1
    device_row = jnp.arange(N_LOCAL, dtype=jnp.int32)[:, None]
    slot_rows = ((device_row * EXPERTS + flat_ids) * CAP + slot_rank).reshape(-1).astype(jnp.int32)
    source_rows = jnp.repeat(normed, TOP, axis=0)
    buffer = jnp.zeros((N_LOCAL * EXPERTS * CAP, D), jnp.bfloat16).at[slot_rows].set(source_rows)
    by_expert = buffer.reshape(N_LOCAL, EXPERTS, CAP, D).transpose(1, 0, 2, 3).reshape(EXPERTS, N_LOCAL * CAP, D)
    split_in = w_in.reshape(EXPERTS, SPLIT, D, HID_DEV)
    split_bias = b_in.reshape(EXPERTS, SPLIT, HID_DEV)
    split_out = w_out.reshape(EXPERTS, SPLIT, HID_DEV, D)
    results = lax.map(one_expert, (by_expert, split_in, split_bias, split_out, b_out))
    returned = results.reshape(EXPERTS, N_LOCAL, CAP, D).transpose(1, 0, 2, 3).reshape(N_LOCAL * EXPERTS * CAP, D)
    picked = returned[slot_rows].reshape(TOKENS, TOP, D)
    mixed_out = tokens.astype(jnp.float32) + lax.optimization_barrier(jnp.sum(gate_weights[:, :, None] * picked, axis=1))
    return mixed_out.astype(jnp.bfloat16)
```

```python
import functools

import jax
import jax.numpy as jnp
from jax import lax
from jax.experimental import pallas as pl
from jax.experimental.pallas import tpu as pltpu
from jax.sharding import PartitionSpec as P


def dispatch_kernel(cap, experts, plane_ref, ids_ref, tokens_ref, gain_ref, bias_ref, *out_refs):
    floats = tokens_ref[...].astype(jnp.float32)
    row_mean = jnp.mean(floats, axis=-1, keepdims=True)
    centered = floats - row_mean
    row_var = jnp.mean(centered * centered, axis=-1, keepdims=True)
    normed = centered * lax.rsqrt(row_var + 1e-05) * gain_ref[...] + bias_ref[...]
    normed = normed.astype(jnp.bfloat16)
    tok = floats.shape[0]
    top = ids_ref.shape[0]
    named = lax.rem(plane_ref[0] + lax.broadcasted_iota(jnp.int32, (8, tok), 0), experts)
    member = named == ids_ref[0:1, :]
    for k in range(1, top):
        member = member | (named == ids_ref[k : k + 1, :])
    member = jnp.where(member, 1.0, 0.0)
    before = lax.broadcasted_iota(jnp.int32, (tok, tok), 0) < lax.broadcasted_iota(jnp.int32, (tok, tok), 1)
    rank = jnp.dot(
        member.astype(jnp.bfloat16),
        jnp.where(before, 1.0, 0.0).astype(jnp.bfloat16),
        preferred_element_type=jnp.float32,
    )
    slot = lax.broadcasted_iota(jnp.int32, (cap, tok), 0).astype(jnp.float32)
    for d in range(experts):
        pick = jnp.where(slot == rank[d : d + 1, :], member[d : d + 1, :], 0.0).astype(jnp.bfloat16)
        out_refs[d][...] = jnp.dot(pick, normed, preferred_element_type=jnp.float32).astype(jnp.bfloat16)


def dispatch(plane, ids, tokens, gain, bias, cap, experts):
    width = tokens.shape[1]
    vmem = pl.BlockSpec(memory_space=pltpu.VMEM)
    return pl.pallas_call(
        functools.partial(dispatch_kernel, cap, experts),
        out_shape=[jax.ShapeDtypeStruct((cap, width), jnp.bfloat16)] * experts,
        in_specs=[pl.BlockSpec(memory_space=pltpu.SMEM)] + [vmem] * 4,
        out_specs=[vmem] * experts,
        name="dispatch",
    )(plane, ids.T, tokens, gain[None, :], bias[None, :])


def combine_kernel(cap, experts, plane_ref, ids_ref, gates_ref, tokens_ref, b_out_ref, *refs):
    row_refs, out_ref = refs[:-1], refs[-1]
    tok, top = ids_ref.shape
    lanes = 128
    named = lax.rem(plane_ref[0] + lax.broadcasted_iota(jnp.int32, (tok, lanes), 1), experts)
    member = jnp.zeros((tok, lanes), jnp.float32)
    gate = jnp.zeros((tok, lanes), jnp.float32)
    for k in range(top):
        hit = named == ids_ref[:, k : k + 1]
        member = jnp.where(hit, 1.0, member)
        gate = jnp.where(hit, gates_ref[:, k : k + 1], gate)
    before = lax.broadcasted_iota(jnp.int32, (tok, tok), 1) < lax.broadcasted_iota(jnp.int32, (tok, tok), 0)
    rank = jnp.dot(
        jnp.where(before, 1.0, 0.0).astype(jnp.bfloat16),
        member.astype(jnp.bfloat16),
        preferred_element_type=jnp.float32,
    )
    slot = lax.broadcasted_iota(jnp.int32, (tok, cap), 1).astype(jnp.float32)
    total = None
    for d in range(experts):
        pick = jnp.where(slot == rank[:, d : d + 1], member[:, d : d + 1], 0.0).astype(jnp.bfloat16)
        rows = jnp.dot(pick, row_refs[d][...], preferred_element_type=jnp.float32)
        bias = b_out_ref[pl.ds(lax.rem(plane_ref[0] + d, experts), 1), :]
        term = gate[:, d : d + 1] * (rows + bias)
        total = term if total is None else total + term
    out_ref[...] = (tokens_ref[...].astype(jnp.float32) + total).astype(jnp.bfloat16)


def combine(plane, ids, gates, tokens, b_out, rows, cap):
    experts = b_out.shape[0]
    vmem = pl.BlockSpec(memory_space=pltpu.VMEM)
    return pl.pallas_call(
        functools.partial(combine_kernel, cap, experts),
        out_shape=jax.ShapeDtypeStruct(tokens.shape, jnp.bfloat16),
        in_specs=[pl.BlockSpec(memory_space=pltpu.SMEM)] + [vmem] * (4 + experts),
        out_specs=vmem,
        name="combine",
    )(plane, ids, gates, tokens, b_out, *rows)


def expert_rows(rows, w_in, b_in, w_out):
    total = None
    for k in range(2):
        hidden = jnp.dot(rows, w_in[k], preferred_element_type=jnp.float32)
        hidden = jnp.maximum(hidden + b_in[k], 0.0).astype(jnp.bfloat16)
        part = jnp.dot(hidden, w_out[k], preferred_element_type=jnp.float32)
        total = part if total is None else total + part
    return total


def local(tokens, expert_ids, gate_weights, norm_gain, norm_bias, w_in, b_in, w_out, b_out):
    tok_dev = tokens.shape[0]
    top_count = expert_ids.shape[1]
    devices = lax.axis_size("local")
    experts = b_out.shape[0]
    shared = devices // experts
    assert shared == 8
    slot_cap = min(
        tok_dev, shared * max(1, (3 * tok_dev * top_count // (2 * experts) + shared - 1) // shared)
    )
    plane = (lax.axis_index("local") // shared).reshape(1).astype(jnp.int32)

    def across(value, bit):
        return lax.ppermute(value, "local", [(i, i ^ bit) for i in range(devices)])

    def along(value, planes):
        return lax.ppermute(value, "local", [(i, (i + planes * shared) % devices) for i in range(devices)])

    w_in, w_out = [w_in[0], across(w_in[0], 1)], [w_out[0], across(w_out[0], 1)]
    b_in = [b_in, across(b_in, 1)]

    blocks = dispatch(plane, expert_ids, tokens, norm_gain, norm_bias, slot_cap, experts)
    results = []
    for d in range(experts):
        near, far = (2, 4) if d % 2 == 0 else (4, 2)
        block = blocks[d] if d == 0 else along(blocks[d], d)
        first = across(block, near)
        second = across(block, far)
        third = across(first, far)
        rows = jnp.concatenate([block, first, second, third])
        part = expert_rows(rows, w_in, b_in, w_out).reshape(4, slot_cap, -1)
        part_first = part[1] + across(part[3].astype(jnp.bfloat16), far).astype(jnp.float32)
        summed = part[0] + across(part_first.astype(jnp.bfloat16), near).astype(jnp.float32)
        summed = summed + across(part[2].astype(jnp.bfloat16), far).astype(jnp.float32)
        summed = summed.astype(jnp.bfloat16)
        results.append(summed if d == 0 else along(summed, -d))
    return combine(plane, expert_ids, gate_weights, tokens, b_out, results, slot_cap)


def solution(mesh):
    in_specs = (
        P(("groups", "local"), None),
        P(("groups", "local"), None),
        P(("groups", "local"), None),
        P(),
        P(),
        P("local", None, None),
        P("local", None),
        P("local", None, None),
        P(),
    )
    out_specs = P(("groups", "local"), None)
    return jax.shard_map(local, mesh=mesh, in_specs=in_specs, out_specs=out_specs, check_vma=False)
```

```python
import functools

import jax
import jax.numpy as jnp
from jax import lax
from jax.experimental import pallas as pl
from jax.experimental.pallas import tpu as pltpu
from jax.sharding import PartitionSpec as P


def in_vmem(value):
    return pltpu.with_memory_space_constraint(value, pltpu.VMEM)


def dispatch_kernel(cap, experts, plane_ref, ids_ref, tokens_ref, gain_ref, bias_ref, *out_refs):
    floats = tokens_ref[...].astype(jnp.float32)
    row_mean = jnp.mean(floats, axis=-1, keepdims=True)
    centered = floats - row_mean
    row_var = jnp.mean(centered * centered, axis=-1, keepdims=True)
    normed = centered * lax.rsqrt(row_var + 1e-05) * gain_ref[...] + bias_ref[...]
    normed = normed.astype(jnp.bfloat16)
    tok = floats.shape[0]
    top = ids_ref.shape[0]
    named = lax.rem(plane_ref[0] + lax.broadcasted_iota(jnp.int32, (8, tok), 0), experts)
    member = named == ids_ref[0:1, :]
    for k in range(1, top):
        member = member | (named == ids_ref[k : k + 1, :])
    member = jnp.where(member, 1.0, 0.0)
    before = lax.broadcasted_iota(jnp.int32, (tok, tok), 0) < lax.broadcasted_iota(jnp.int32, (tok, tok), 1)
    rank = jnp.dot(
        member.astype(jnp.bfloat16),
        jnp.where(before, 1.0, 0.0).astype(jnp.bfloat16),
        preferred_element_type=jnp.float32,
    )
    slot = lax.broadcasted_iota(jnp.int32, (cap, tok), 0).astype(jnp.float32)
    for d in range(experts):
        pick = jnp.where(slot == rank[d : d + 1, :], member[d : d + 1, :], 0.0).astype(jnp.bfloat16)
        out_refs[d][...] = jnp.dot(pick, normed, preferred_element_type=jnp.float32).astype(jnp.bfloat16)


def dispatch(plane, ids, tokens, gain, bias, cap, experts):
    width = tokens.shape[1]
    vmem = pl.BlockSpec(memory_space=pltpu.VMEM)
    return pl.pallas_call(
        functools.partial(dispatch_kernel, cap, experts),
        out_shape=[pltpu.VMEM((cap, width), jnp.bfloat16)] * experts,
        in_specs=[pl.BlockSpec(memory_space=pltpu.SMEM)] + [vmem] * 4,
        out_specs=[vmem] * experts,
        compiler_params=pltpu.CompilerParams(vmem_limit_bytes=8 << 20),
        name="dispatch",
    )(plane, ids.T, tokens, gain[None, :], bias[None, :])


def combine_kernel(cap, experts, plane_ref, ids_ref, gates_ref, tokens_ref, b_out_ref, *refs):
    row_refs, out_ref = refs[:-1], refs[-1]
    tok, top = ids_ref.shape
    lanes = 128
    named = lax.rem(plane_ref[0] + lax.broadcasted_iota(jnp.int32, (tok, lanes), 1), experts)
    member = jnp.zeros((tok, lanes), jnp.float32)
    gate = jnp.zeros((tok, lanes), jnp.float32)
    for k in range(top):
        hit = named == ids_ref[:, k : k + 1]
        member = jnp.where(hit, 1.0, member)
        gate = jnp.where(hit, gates_ref[:, k : k + 1], gate)
    before = lax.broadcasted_iota(jnp.int32, (tok, tok), 1) < lax.broadcasted_iota(jnp.int32, (tok, tok), 0)
    rank = jnp.dot(
        jnp.where(before, 1.0, 0.0).astype(jnp.bfloat16),
        member.astype(jnp.bfloat16),
        preferred_element_type=jnp.float32,
    )
    slot = lax.broadcasted_iota(jnp.int32, (tok, cap), 1).astype(jnp.float32)
    total = None
    for d in range(experts):
        pick = jnp.where(slot == rank[:, d : d + 1], member[:, d : d + 1], 0.0).astype(jnp.bfloat16)
        rows = jnp.dot(pick, row_refs[d][...], preferred_element_type=jnp.float32)
        bias = b_out_ref[pl.ds(lax.rem(plane_ref[0] + d, experts), 1), :]
        term = gate[:, d : d + 1] * (rows + bias)
        total = term if total is None else total + term
    out_ref[...] = (tokens_ref[...].astype(jnp.float32) + total).astype(jnp.bfloat16)


def combine(plane, ids, gates, tokens, b_out, rows, cap):
    experts = b_out.shape[0]
    vmem = pl.BlockSpec(memory_space=pltpu.VMEM)
    return pl.pallas_call(
        functools.partial(combine_kernel, cap, experts),
        out_shape=jax.ShapeDtypeStruct(tokens.shape, jnp.bfloat16),
        in_specs=[pl.BlockSpec(memory_space=pltpu.SMEM)] + [vmem] * (4 + experts),
        out_specs=vmem,
        compiler_params=pltpu.CompilerParams(vmem_limit_bytes=8 << 20),
        name="combine",
    )(plane, ids, gates, in_vmem(tokens), b_out, *[in_vmem(value) for value in rows])


def expert_kernel(tile, *refs):
    blocks = (len(refs) - 8) // 2
    row_refs, (in_0, in_1, bias_0, bias_1, out_0, out_1) = refs[:blocks], refs[blocks : blocks + 6]
    part_refs, (rows, hidden) = refs[blocks + 6 : -2], refs[-2:]
    cap = row_refs[0].shape[0]
    units = in_0.shape[1]
    for b in range(blocks):
        rows[b * cap : (b + 1) * cap, :] = row_refs[b][...]
    for k, (w_in, bias) in enumerate(((in_0, bias_0), (in_1, bias_1))):
        for start in range(0, units, tile):
            cols = slice(start, start + tile)
            sums = jnp.dot(rows[...], w_in[:, cols], preferred_element_type=jnp.float32) + bias[:, cols]
            hidden[:, k * units + start : k * units + start + tile] = jnp.maximum(sums, 0.0).astype(jnp.bfloat16)
    for start in range(0, out_0.shape[1], tile):
        cols = slice(start, start + tile)
        sums = jnp.dot(hidden[:, :units], out_0[:, cols], preferred_element_type=jnp.float32)
        sums += jnp.dot(hidden[:, units:], out_1[:, cols], preferred_element_type=jnp.float32)
        for b in range(blocks):
            part_refs[b][:, cols] = sums[b * cap : (b + 1) * cap, :].astype(part_refs[b].dtype)


def expert_rows(rows, weights, types):
    cap, width = rows[0].shape
    units = weights[0].shape[1]
    count = len(rows) * cap
    vmem = pl.BlockSpec(memory_space=pltpu.VMEM)
    return pl.pallas_call(
        functools.partial(expert_kernel, 512),
        out_shape=[pltpu.VMEM((cap, width), kind) for kind in types],
        in_specs=[vmem] * (len(rows) + 6),
        out_specs=[vmem] * len(rows),
        scratch_shapes=[pltpu.VMEM((count, width), jnp.bfloat16), pltpu.VMEM((count, 2 * units), jnp.bfloat16)],
        compiler_params=pltpu.CompilerParams(vmem_limit_bytes=12 << 20),
        cost_estimate=pl.CostEstimate(
            flops=8 * count * width * units, bytes_accessed=8 * width * units, transcendentals=0
        ),
        name="expert",
    )(*[in_vmem(value) for value in (*rows, *weights)])


def local(tokens, expert_ids, gate_weights, norm_gain, norm_bias, w_in, b_in, w_out, b_out):
    tok_dev = tokens.shape[0]
    top_count = expert_ids.shape[1]
    devices = lax.axis_size("local")
    experts = b_out.shape[0]
    shared = devices // experts
    assert shared == 8
    slot_cap = min(
        tok_dev, shared * max(1, (3 * tok_dev * top_count // (2 * experts) + shared - 1) // shared)
    )
    slot_cap += -slot_cap % 16
    plane = (lax.axis_index("local") // shared).reshape(1).astype(jnp.int32)

    def across(value, bit):
        return lax.ppermute(value, "local", [(i, i ^ bit) for i in range(devices)])

    def along(value, planes):
        return lax.ppermute(value, "local", [(i, (i + planes * shared) % devices) for i in range(devices)])

    w_in, w_out = w_in[0], w_out[0]
    weights = (w_in, across(w_in, 1), b_in, across(b_in, 1), w_out, across(w_out, 1))
    kinds = (jnp.float32, jnp.float32, jnp.bfloat16, jnp.bfloat16)

    blocks = dispatch(plane, expert_ids, tokens, norm_gain, norm_bias, slot_cap, experts)
    results = []
    for d in range(experts):
        near, far = (2, 4) if d % 2 == 0 else (4, 2)
        block = blocks[d] if d == 0 else along(blocks[d], d)
        first = across(block, near)
        second = across(block, far)
        third = across(first, far)
        part = expert_rows([block, first, second, third], weights, kinds)
        part_first = part[1] + across(part[3], far).astype(jnp.float32)
        summed = part[0] + across(part_first.astype(jnp.bfloat16), near).astype(jnp.float32)
        summed = (summed + across(part[2], far).astype(jnp.float32)).astype(jnp.bfloat16)
        results.append(summed if d == 0 else along(summed, -d))
    return combine(plane, expert_ids, gate_weights, tokens, b_out, results, slot_cap)


def solution(mesh):
    in_specs = (
        P(("groups", "local"), None),
        P(("groups", "local"), None),
        P(("groups", "local"), None),
        P(),
        P(),
        P("local", None, None),
        P("local", None),
        P("local", None, None),
        P(),
    )
    out_specs = P(("groups", "local"), None)
    return jax.shard_map(local, mesh=mesh, in_specs=in_specs, out_specs=out_specs, check_vma=False)
```

```python
import functools

import jax
import jax.numpy as jnp
from jax import lax
from jax.experimental import pallas as pl
from jax.experimental.pallas import tpu as pltpu
from jax.sharding import PartitionSpec as P


def in_vmem(value):
    return pltpu.with_memory_space_constraint(value, pltpu.VMEM)


def in_hbm(value):
    return pltpu.with_memory_space_constraint(value, pltpu.HBM)


def dispatch_kernel(cap, experts, plane_ref, ids_ref, tokens_ref, gain_ref, bias_ref, *out_refs):
    floats = tokens_ref[...].astype(jnp.float32)
    row_mean = jnp.mean(floats, axis=-1, keepdims=True)
    centered = floats - row_mean
    row_var = jnp.mean(centered * centered, axis=-1, keepdims=True)
    normed = centered * lax.rsqrt(row_var + 1e-05) * gain_ref[...] + bias_ref[...]
    normed = normed.astype(jnp.bfloat16)
    tok = floats.shape[0]
    top = ids_ref.shape[0]
    named = lax.rem(plane_ref[0] + lax.broadcasted_iota(jnp.int32, (8, tok), 0), experts)
    member = named == ids_ref[0:1, :]
    for k in range(1, top):
        member = member | (named == ids_ref[k : k + 1, :])
    member = jnp.where(member, 1.0, 0.0)
    before = lax.broadcasted_iota(jnp.int32, (tok, tok), 0) < lax.broadcasted_iota(jnp.int32, (tok, tok), 1)
    rank = jnp.dot(
        member.astype(jnp.bfloat16),
        jnp.where(before, 1.0, 0.0).astype(jnp.bfloat16),
        preferred_element_type=jnp.float32,
    )
    slot = lax.broadcasted_iota(jnp.int32, (cap, tok), 0).astype(jnp.float32)
    for d in range(experts):
        pick = jnp.where(slot == rank[d : d + 1, :], member[d : d + 1, :], 0.0).astype(jnp.bfloat16)
        out_refs[d][...] = jnp.dot(pick, normed, preferred_element_type=jnp.float32).astype(jnp.bfloat16)


def dispatch(plane, ids, tokens, gain, bias, cap, experts):
    width = tokens.shape[1]
    vmem = pl.BlockSpec(memory_space=pltpu.VMEM)
    return pl.pallas_call(
        functools.partial(dispatch_kernel, cap, experts),
        out_shape=[pltpu.VMEM((cap, width), jnp.bfloat16)] * experts,
        in_specs=[pl.BlockSpec(memory_space=pltpu.SMEM)] + [vmem] * 4,
        out_specs=[vmem] * experts,
        compiler_params=pltpu.CompilerParams(vmem_limit_bytes=8 << 20),
        name="dispatch",
    )(plane, in_hbm(ids.T), in_hbm(tokens), in_hbm(gain[None, :]), in_hbm(bias[None, :]))


def combine_kernel(cap, experts, plane_ref, ids_ref, gates_ref, tokens_ref, b_out_ref, *refs):
    row_refs, out_ref = refs[:-1], refs[-1]
    top, tok = ids_ref.shape
    named = lax.rem(plane_ref[0] + lax.broadcasted_iota(jnp.int32, (8, tok), 0), experts)
    member = jnp.zeros((8, tok), jnp.float32)
    gate = jnp.zeros((8, tok), jnp.float32)
    for k in range(top):
        hit = named == ids_ref[k : k + 1, :]
        member = jnp.where(hit, 1.0, member)
        gate = jnp.where(hit, gates_ref[k : k + 1, :], gate)
    row, column = (lax.broadcasted_iota(jnp.int32, (tok, tok), axis) for axis in (0, 1))
    rank = jnp.dot(
        member.astype(jnp.bfloat16),
        jnp.where(row < column, 1.0, 0.0).astype(jnp.bfloat16),
        preferred_element_type=jnp.float32,
    )
    rank = jnp.where(member > 0.0, rank, -1.0)
    turn = jnp.where(row == column, 1.0, 0.0)
    flip = functools.partial(
        lax.dot_general,
        turn,
        dimension_numbers=(((1,), (1,)), ((), ())),
        precision=lax.Precision.HIGHEST,
        preferred_element_type=jnp.float32,
    )
    rank, gate = flip(rank), flip(gate)
    slot = lax.broadcasted_iota(jnp.int32, (tok, cap), 1).astype(jnp.float32)
    total = None
    for d in range(experts):
        pick = jnp.where(slot == rank[:, d : d + 1], 1.0, 0.0).astype(jnp.bfloat16)
        rows = jnp.dot(pick, row_refs[d][...], preferred_element_type=jnp.float32)
        bias = b_out_ref[pl.ds(lax.rem(plane_ref[0] + d, experts), 1), :]
        term = gate[:, d : d + 1] * (rows + bias)
        total = term if total is None else total + term
    out_ref[...] = (tokens_ref[...].astype(jnp.float32) + total).astype(jnp.bfloat16)


def combine(plane, ids, gates, tokens, b_out, rows, cap):
    experts = b_out.shape[0]
    vmem = pl.BlockSpec(memory_space=pltpu.VMEM)
    return pl.pallas_call(
        functools.partial(combine_kernel, cap, experts),
        out_shape=jax.ShapeDtypeStruct(tokens.shape, jnp.bfloat16),
        in_specs=[pl.BlockSpec(memory_space=pltpu.SMEM)] + [vmem] * (4 + experts),
        out_specs=vmem,
        compiler_params=pltpu.CompilerParams(vmem_limit_bytes=8 << 20),
        name="combine",
    )(plane, ids.T, gates.T, in_vmem(tokens), b_out, *[in_vmem(value) for value in rows])


def after(value, *earlier):
    return lax.optimization_barrier((value, *earlier))[0]


def stage_kernel(*refs):
    count = len(refs) // 3
    sources, targets, sems = refs[:count], refs[count : 2 * count], refs[2 * count :]
    copies = [pltpu.make_async_copy(*three) for three in zip(sources, targets, sems)]
    for copy in copies:
        copy.start()
    for copy in copies:
        copy.wait()


def stage(*arrays):
    return pl.pallas_call(
        stage_kernel,
        out_shape=[pltpu.VMEM(array.shape, array.dtype) for array in arrays],
        in_specs=[pl.BlockSpec(memory_space=pl.ANY)] * len(arrays),
        out_specs=[pl.BlockSpec(memory_space=pltpu.VMEM)] * len(arrays),
        scratch_shapes=[pltpu.SemaphoreType.DMA] * len(arrays),
        compiler_params=pltpu.CompilerParams(vmem_limit_bytes=4 << 20),
        name="stage",
    )(*[in_hbm(array) for array in arrays])


def expert_kernel(tile, *refs):
    blocks = (len(refs) - 8) // 2
    row_refs, (in_0, in_1, bias_0, bias_1, out_0, out_1) = refs[:blocks], refs[blocks : blocks + 6]
    part_refs, (rows, hidden) = refs[blocks + 6 : -2], refs[-2:]
    cap = row_refs[0].shape[0]
    units = in_0.shape[1]
    for b in range(blocks):
        rows[b * cap : (b + 1) * cap, :] = row_refs[b][...]
    for k, (w_in, bias) in enumerate(((in_0, bias_0), (in_1, bias_1))):
        for start in range(0, units, tile):
            cols = slice(start, start + tile)
            sums = jnp.dot(rows[...], w_in[:, cols], preferred_element_type=jnp.float32) + bias[:, cols]
            hidden[:, k * units + start : k * units + start + tile] = jnp.maximum(sums, 0.0).astype(jnp.bfloat16)
    for start in range(0, out_0.shape[1], tile):
        cols = slice(start, start + tile)
        sums = jnp.dot(hidden[:, :units], out_0[:, cols], preferred_element_type=jnp.float32)
        sums += jnp.dot(hidden[:, units:], out_1[:, cols], preferred_element_type=jnp.float32)
        for b in range(blocks):
            part_refs[b][:, cols] = sums[b * cap : (b + 1) * cap, :].astype(part_refs[b].dtype)


def expert_rows(rows, weights, types):
    cap, width = rows[0].shape
    units = weights[0].shape[1]
    count = len(rows) * cap
    vmem = pl.BlockSpec(memory_space=pltpu.VMEM)
    return pl.pallas_call(
        functools.partial(expert_kernel, 512),
        out_shape=[pltpu.VMEM((cap, width), kind) for kind in types],
        in_specs=[vmem] * (len(rows) + 6),
        out_specs=[vmem] * len(rows),
        scratch_shapes=[pltpu.VMEM((count, width), jnp.bfloat16), pltpu.VMEM((count, 2 * units), jnp.bfloat16)],
        compiler_params=pltpu.CompilerParams(vmem_limit_bytes=12 << 20),
        cost_estimate=pl.CostEstimate(
            flops=8 * count * width * units, bytes_accessed=8 * width * units, transcendentals=0
        ),
        name="expert",
    )(*[in_vmem(value) for value in (*rows, *weights)])


def local(tokens, expert_ids, gate_weights, norm_gain, norm_bias, w_in, b_in, w_out, b_out):
    tok_dev = tokens.shape[0]
    top_count = expert_ids.shape[1]
    devices = lax.axis_size("local")
    experts = b_out.shape[0]
    shared = devices // experts
    assert shared == 8
    slot_cap = min(
        tok_dev, shared * max(1, (3 * tok_dev * top_count // (2 * experts) + shared - 1) // shared)
    )
    slot_cap += -slot_cap % 16
    plane = (lax.axis_index("local") // shared).reshape(1).astype(jnp.int32)

    def across(value, bit):
        return lax.ppermute(value, "local", [(i, i ^ bit) for i in range(devices)])

    def along(value, planes):
        return lax.ppermute(value, "local", [(i, (i + planes * shared) % devices) for i in range(devices)])

    w_in, w_out = w_in[0], w_out[0]
    kinds = (jnp.float32, jnp.float32, jnp.bfloat16, jnp.bfloat16)
    peer_in, peer_out, peer_bias = across(w_in, 1), across(w_out, 1), across(b_in, 1)

    blocks = dispatch(plane, expert_ids, tokens, norm_gain, norm_bias, slot_cap, experts)
    mark = [None]

    def then(*values):
        if mark[0] is not None:
            values = lax.optimization_barrier((*values, mark[0]))[:-1]
        mark[0] = values[0]
        return values if len(values) > 1 else values[0]

    class Block:
        def __init__(self, d, near, far):
            self.d, self.near, self.far = d, near, far

        def spread(self, rows):
            self.rows = rows
            self.first, self.second = across(rows, self.near), across(rows, self.far)

        def pass_on(self):
            self.first = then(self.first)
            self.third = across(self.first, self.far)

        def compute(self):
            rows = then(self.rows, self.first, self.second, self.third)
            self.part = expert_rows(rows, weights, kinds)
            self.back_third = across(self.part[3], self.far)
            self.back_second = across(self.part[2], self.far)

        def fold(self):
            self.back_third = then(self.back_third)
            both = self.part[1] + self.back_third.astype(jnp.float32)
            self.back_first = across(both.astype(jnp.bfloat16), self.near)

        def finish(self):
            first, second = then(self.back_first, self.back_second)
            summed = self.part[0] + first.astype(jnp.float32) + second.astype(jnp.float32)
            self.out = summed.astype(jnp.bfloat16)
            if self.d:
                self.out = along(self.out, -self.d)

    order = [0] + sorted(range(1, experts), key=lambda d: min(d, experts - d))
    units = [Block(d, *((2, 4) if i % 2 == 0 else (4, 2))) for i, d in enumerate(order)]
    own, rest = units[0], units[1:]
    moved = {}
    for unit in rest:
        steps = min(unit.d, experts - unit.d)
        moved[unit.d] = [along(blocks[unit.d], 1 if unit.d == steps else -1), steps - 1]
    own.spread(blocks[0])
    weights = None
    for turn in range(experts):
        for unit in rest:
            if unit.d in moved:
                value, left = moved[unit.d]
                value = then(value)
                if left:
                    moved[unit.d] = [along(value, 1 if 2 * unit.d <= experts else -1), left - 1]
                else:
                    del moved[unit.d]
                    unit.spread(value)
                    if unit is rest[0]:
                        own.pass_on()
                    else:
                        rest[rest.index(unit) - 1].pass_on()
        if turn == 0:
            w_in, w_out = stage(then(w_in), w_out)
    peer_in, peer_out = stage(then(peer_in), peer_out)
    weights = (w_in, peer_in, b_in, peer_bias, w_out, peer_out)
    rest[0].compute()
    rest[-1].pass_on()
    for i, unit in enumerate(rest[1:] + [own]):
        unit.compute()
        units[i + 1].fold()
    for i, unit in enumerate(rest):
        unit.finish()
        if i == 0:
            own.fold()
    own.finish()
    results = [next(unit.out for unit in units if unit.d == d) for d in range(experts)]
    return combine(plane, expert_ids, gate_weights, tokens, b_out, results, slot_cap)


def solution(mesh):
    in_specs = (
        P(("groups", "local"), None),
        P(("groups", "local"), None),
        P(("groups", "local"), None),
        P(),
        P(),
        P("local", None, None),
        P("local", None),
        P("local", None, None),
        P(),
    )
    out_specs = P(("groups", "local"), None)
    return jax.shard_map(local, mesh=mesh, in_specs=in_specs, out_specs=out_specs, check_vma=False)
```

```python
import functools

import jax
import jax.numpy as jnp
from jax import lax
from jax.experimental import pallas as pl
from jax.experimental.pallas import tpu as pltpu
from jax.sharding import PartitionSpec as P


def in_vmem(value):
    return pltpu.with_memory_space_constraint(value, pltpu.VMEM)


def in_hbm(value):
    return pltpu.with_memory_space_constraint(value, pltpu.HBM)


def dispatch_kernel(cap, experts, plane_ref, ids_ref, tokens_ref, gain_ref, bias_ref, *out_refs):
    floats = tokens_ref[...].astype(jnp.float32)
    row_mean = jnp.mean(floats, axis=-1, keepdims=True)
    centered = floats - row_mean
    row_var = jnp.mean(centered * centered, axis=-1, keepdims=True)
    normed = centered * lax.rsqrt(row_var + 1e-05) * gain_ref[...] + bias_ref[...]
    normed = normed.astype(jnp.bfloat16)
    tok = floats.shape[0]
    top = ids_ref.shape[0]
    named = lax.rem(plane_ref[0] + lax.broadcasted_iota(jnp.int32, (8, tok), 0), experts)
    member = named == ids_ref[0:1, :]
    for k in range(1, top):
        member = member | (named == ids_ref[k : k + 1, :])
    member = jnp.where(member, 1.0, 0.0)
    before = lax.broadcasted_iota(jnp.int32, (tok, tok), 0) < lax.broadcasted_iota(jnp.int32, (tok, tok), 1)
    rank = jnp.dot(
        member.astype(jnp.bfloat16),
        jnp.where(before, 1.0, 0.0).astype(jnp.bfloat16),
        preferred_element_type=jnp.float32,
    )
    slot = lax.broadcasted_iota(jnp.int32, (cap, tok), 0).astype(jnp.float32)
    for d in range(experts):
        pick = jnp.where(slot == rank[d : d + 1, :], member[d : d + 1, :], 0.0).astype(jnp.bfloat16)
        out_refs[d][...] = jnp.dot(pick, normed, preferred_element_type=jnp.float32).astype(jnp.bfloat16)


def dispatch(plane, ids, tokens, gain, bias, cap, experts):
    width = tokens.shape[1]
    vmem = pl.BlockSpec(memory_space=pltpu.VMEM)
    return pl.pallas_call(
        functools.partial(dispatch_kernel, cap, experts),
        out_shape=[pltpu.VMEM((cap, width), jnp.bfloat16)] * experts,
        in_specs=[pl.BlockSpec(memory_space=pltpu.SMEM)] + [vmem] * 4,
        out_specs=[vmem] * experts,
        compiler_params=pltpu.CompilerParams(vmem_limit_bytes=8 << 20),
        name="dispatch",
    )(plane, in_hbm(ids.T), in_hbm(tokens), in_hbm(gain[None, :]), in_hbm(bias[None, :]))


def combine_kernel(cap, experts, plane_ref, ids_ref, gates_ref, tokens_ref, b_out_ref, *refs):
    row_refs, out_ref = refs[:-1], refs[-1]
    top, tok = ids_ref.shape
    named = lax.rem(plane_ref[0] + lax.broadcasted_iota(jnp.int32, (8, tok), 0), experts)
    member = jnp.zeros((8, tok), jnp.float32)
    gate = jnp.zeros((8, tok), jnp.float32)
    for k in range(top):
        hit = named == ids_ref[k : k + 1, :]
        member = jnp.where(hit, 1.0, member)
        gate = jnp.where(hit, gates_ref[k : k + 1, :], gate)
    row, column = (lax.broadcasted_iota(jnp.int32, (tok, tok), axis) for axis in (0, 1))
    rank = jnp.dot(
        member.astype(jnp.bfloat16),
        jnp.where(row < column, 1.0, 0.0).astype(jnp.bfloat16),
        preferred_element_type=jnp.float32,
    )
    rank = jnp.where(member > 0.0, rank, -1.0)
    turn = jnp.where(row == column, 1.0, 0.0)
    flip = functools.partial(
        lax.dot_general,
        turn,
        dimension_numbers=(((1,), (1,)), ((), ())),
        precision=lax.Precision.HIGHEST,
        preferred_element_type=jnp.float32,
    )
    rank, gate = flip(rank), flip(gate)
    slot = lax.broadcasted_iota(jnp.int32, (tok, cap), 1).astype(jnp.float32)
    total = None
    for d in range(experts):
        pick = jnp.where(slot == rank[:, d : d + 1], 1.0, 0.0).astype(jnp.bfloat16)
        rows = jnp.dot(pick, row_refs[d][...], preferred_element_type=jnp.float32)
        bias = b_out_ref[pl.ds(lax.rem(plane_ref[0] + d, experts), 1), :]
        term = gate[:, d : d + 1] * (rows + bias)
        total = term if total is None else total + term
    out_ref[...] = (tokens_ref[...].astype(jnp.float32) + total).astype(jnp.bfloat16)


def combine(plane, ids, gates, tokens, b_out, rows, cap):
    experts = b_out.shape[0]
    vmem = pl.BlockSpec(memory_space=pltpu.VMEM)
    return pl.pallas_call(
        functools.partial(combine_kernel, cap, experts),
        out_shape=jax.ShapeDtypeStruct(tokens.shape, jnp.bfloat16),
        in_specs=[pl.BlockSpec(memory_space=pltpu.SMEM)] + [vmem] * (4 + experts),
        out_specs=vmem,
        compiler_params=pltpu.CompilerParams(vmem_limit_bytes=8 << 20),
        name="combine",
    )(plane, ids.T, gates.T, in_vmem(tokens), b_out, *[in_vmem(value) for value in rows])


def stage_kernel(*refs):
    count = len(refs) // 3
    sources, targets, sems = refs[:count], refs[count : 2 * count], refs[2 * count :]
    copies = [pltpu.make_async_copy(*three) for three in zip(sources, targets, sems)]
    for copy in copies:
        copy.start()
    for copy in copies:
        copy.wait()


def stage(*arrays):
    return pl.pallas_call(
        stage_kernel,
        out_shape=[pltpu.VMEM(array.shape, array.dtype) for array in arrays],
        in_specs=[pl.BlockSpec(memory_space=pl.ANY)] * len(arrays),
        out_specs=[pl.BlockSpec(memory_space=pltpu.VMEM)] * len(arrays),
        scratch_shapes=[pltpu.SemaphoreType.DMA] * len(arrays),
        compiler_params=pltpu.CompilerParams(vmem_limit_bytes=4 << 20),
        name="stage",
    )(*[in_hbm(array) for array in arrays])


def feed_forward(count, tile, weights, rows, hidden, put):
    in_0, in_1, bias_0, bias_1, out_0, out_1 = weights
    units, width = out_0.shape
    for k, (w_in, bias) in enumerate(((in_0, bias_0), (in_1, bias_1))):
        for t in range(units // tile):
            cols = slice(t * tile, (t + 1) * tile)
            sums = jnp.dot(rows[...], w_in[:, cols], preferred_element_type=jnp.float32) + bias[:, cols]
            hidden[:, k * units + t * tile : k * units + (t + 1) * tile] = jnp.maximum(sums, 0.0).astype(jnp.bfloat16)
    for t in range(width // tile):
        cols = slice(t * tile, (t + 1) * tile)
        sums = jnp.dot(hidden[:, :units], out_0[:, cols], preferred_element_type=jnp.float32)
        sums += jnp.dot(hidden[:, units:], out_1[:, cols], preferred_element_type=jnp.float32)
        put(t * tile, (t + 1) * tile, sums)


def expert_kernel(tile, *refs):
    pieces = (len(refs) - 8) // 2
    row_refs, weights, sum_refs, (rows, hidden) = refs[:pieces], refs[pieces : pieces + 6], refs[pieces + 6 : -2], refs[-2:]
    count = row_refs[0].shape[0]
    width = rows.shape[1]
    places = []
    start = column = 0
    for ref in row_refs:
        places.append((start, column))
        rows[start : start + count, column : column + ref.shape[1]] = ref[...]
        column = (column + ref.shape[1]) % width
        start += 0 if column else count

    def put(first, last, sums):
        for ref, (start, column) in zip(sum_refs, places):
            if column <= first < column + ref.shape[1]:
                piece = sums[start : start + count, :].astype(ref.dtype)
                ref[:, first - column : last - column] = piece

    feed_forward(count, tile, weights, rows, hidden, put)


def expert_rows(rows, weights, kinds):
    count, width = rows[0].shape[0], weights[0].shape[0]
    units = weights[0].shape[1]
    total = count * sum(value.shape[1] for value in rows) // width
    vmem = pl.BlockSpec(memory_space=pltpu.VMEM)
    return pl.pallas_call(
        functools.partial(expert_kernel, 512),
        out_shape=[pltpu.VMEM(value.shape, kind) for value, kind in zip(rows, kinds)],
        in_specs=[vmem] * (len(rows) + 6),
        out_specs=[vmem] * len(rows),
        scratch_shapes=[pltpu.VMEM((total, width), jnp.bfloat16), pltpu.VMEM((total, 2 * units), jnp.bfloat16)],
        compiler_params=pltpu.CompilerParams(vmem_limit_bytes=16 << 20),
        name="expert",
    )(*[in_vmem(value) for value in (*rows, *weights)])


def local(tokens, expert_ids, gate_weights, norm_gain, norm_bias, w_in, b_in, w_out, b_out):
    tok_dev = tokens.shape[0]
    top_count = expert_ids.shape[1]
    devices = lax.axis_size("local")
    experts = b_out.shape[0]
    shared = devices // experts
    assert shared == 8
    slot_cap = min(
        tok_dev, shared * max(1, (3 * tok_dev * top_count // (2 * experts) + shared - 1) // shared)
    )
    slot_cap += -slot_cap % 16
    plane = (lax.axis_index("local") // shared).reshape(1).astype(jnp.int32)

    def across(value, bit):
        return lax.ppermute(value, "local", [(i, i ^ bit) for i in range(devices)])

    def along(value, planes):
        return lax.ppermute(value, "local", [(i, (i + planes * shared) % devices) for i in range(devices)])

    w_in, w_out = w_in[0], w_out[0]
    half = tokens.shape[1] // 2
    sent = {}

    def put(name, make, *args):
        with jax.named_scope(name):
            sent[name] = make(*args)

    def join(*names, ordered=()):
        for early, late in zip(ordered, ordered[1:]):
            sent[late] = lax.optimization_barrier((sent[late], sent[early]))[0]
        names += ordered
        values = lax.optimization_barrier([sent[name] for name in names])
        sent.update(zip(names, values))

    def fold(sums, low, high):
        to_x = jnp.concatenate([sums[1][:, :half] + low.astype(jnp.float32), sums[1][:, half:]], axis=1)
        to_y = jnp.concatenate([sums[2][:, :half], sums[2][:, half:] + high.astype(jnp.float32)], axis=1)
        return to_x.astype(jnp.bfloat16), to_y.astype(jnp.bfloat16)

    def total(sums, *others):
        return (sums[0] + sum(value.astype(jnp.float32) for value in others)).astype(jnp.bfloat16)

    near = sorted({1, experts - 1})
    far = list(range(2, experts - 1))
    wide, short = jnp.float32, jnp.bfloat16
    blocks = dispatch(plane, expert_ids, tokens, norm_gain, norm_bias, slot_cap, experts)
    own = blocks[0]
    put("w1", across, w_in, 1)
    put("z1", along, blocks[near[0]], near[0])
    put("z3", along, blocks[near[-1]], near[-1])
    put("ox", across, own, 2)
    put("oy", across, own, 4)
    put("od", across, own, 6)
    sent["mine"], sent["own"] = [w_in, w_out], own
    join("mine", "own")
    put("K", stage, *sent["mine"])
    sent["out"], sent["bias"], sent["blocks"] = w_out, b_in, [blocks[d] for d in far]
    join("own", "out", "bias", "blocks", ordered=("z1", "z3", "ox", "oy", "w1", "K"))
    mine_in, mine_out = sent["K"]
    near_rows = jnp.concatenate([sent["z1"], sent["z3"]][: len(near)])
    put("w2", across, sent["out"], 1)
    put("A1x", across, near_rows, 2)
    put("A1y", across, near_rows, 4)
    put("z2", lambda: [along(block, d) for block, d in zip(sent["blocks"], far)])
    put("b", across, sent["bias"], 1)
    put("K2", stage, sent["w1"], sent["w2"])
    join("A1x", "A1y", "K2", "b")
    peer_in, peer_out = sent["K2"]
    weights = (mine_in, peer_in, b_in, sent["b"], mine_out, peer_out)
    far_rows = jnp.concatenate(sent["z2"]) if len(far) > 1 else sent["z2"][0]
    put("A2a", across, sent["A1x"][:, :half], 4)
    put("A2b", across, sent["A1y"][:, half:], 2)
    put("B1x", across, far_rows, 2)
    put("B1y", across, far_rows, 4)
    put("bd", across, far_rows, 6)
    put("EA1", expert_rows, [near_rows, sent["A1x"], sent["A1y"]], weights, [wide] * 3)
    join("EA1", "A2a", "A2b", "od")
    put("EA2", expert_rows, [sent["A2a"], sent["A2b"]], weights, [short] * 2)
    join("EA2", "B1x", "B1y")
    put("AR1a", across, sent["EA2"][0], 4)
    put("AR1b", across, sent["EA2"][1], 2)
    rows = [far_rows, *(sent[name] for name in ("B1x", "B1y", "bd"))]
    put("EB", expert_rows, rows, weights, [wide] + [short] * 3)
    join("EB", "AR1a", "AR1b")
    to_x, to_y = fold(sent["EA1"], sent["AR1a"], sent["AR1b"])
    put("AR2x", across, to_x, 2)
    put("AR2y", across, to_y, 4)
    for part, piece, bits in zip("xyd", sent["EB"][1:], (2, 4, 6)):
        put("BR" + part, across, piece, bits)
    rows = [sent["own"], sent["ox"], sent["oy"], sent["od"]]
    rows, sent["EB"] = lax.optimization_barrier((rows, list(sent["EB"])))
    put("EO", expert_rows, rows, weights, [wide] + [short] * 3)
    join("AR2x", "AR2y", "EO")
    value = total(sent["EA1"], sent["AR2x"], sent["AR2y"])
    for i, d in enumerate(near):
        put("c1" if i == 0 else "c3", along, value[i * slot_cap : (i + 1) * slot_cap], -d)
    join("BRx", "BRy", "BRd")
    value = total(sent["EB"], *(sent[name] for name in ("BRx", "BRy", "BRd")))
    put("c2", lambda: [along(value[i * slot_cap : (i + 1) * slot_cap], -d) for i, d in enumerate(far)])
    for part, piece, bits in zip("xyd", sent["EO"][1:], (2, 4, 6)):
        put("OR" + part, across, piece, bits)
    rows = dict(zip(far, sent["c2"]))
    rows[near[0]], rows[near[-1]] = sent["c1"], sent["c3"]
    rows[0] = total(sent["EO"], sent["ORx"], sent["ORy"], sent["ORd"])
    results = [rows[d] for d in range(experts)]
    return combine(plane, expert_ids, gate_weights, tokens, b_out, results, slot_cap)


def solution(mesh):
    in_specs = (
        P(("groups", "local"), None),
        P(("groups", "local"), None),
        P(("groups", "local"), None),
        P(),
        P(),
        P("local", None, None),
        P("local", None),
        P("local", None, None),
        P(),
    )
    out_specs = P(("groups", "local"), None)
    return jax.shard_map(local, mesh=mesh, in_specs=in_specs, out_specs=out_specs, check_vma=False)
```

```python
import functools

import jax
import jax.numpy as jnp
from jax import lax
from jax.experimental import pallas as pl
from jax.experimental.pallas import tpu as pltpu
from jax.sharding import PartitionSpec as P


def in_vmem(value):
    return pltpu.with_memory_space_constraint(value, pltpu.VMEM)


def in_hbm(value):
    return pltpu.with_memory_space_constraint(value, pltpu.HBM)


def dispatch_kernel(cap, experts, plane_ref, ids_ref, tokens_ref, gain_ref, bias_ref, *out_refs):
    floats = tokens_ref[...].astype(jnp.float32)
    row_mean = jnp.mean(floats, axis=-1, keepdims=True)
    centered = floats - row_mean
    row_var = jnp.mean(centered * centered, axis=-1, keepdims=True)
    normed = centered * lax.rsqrt(row_var + 1e-05) * gain_ref[...] + bias_ref[...]
    normed = normed.astype(jnp.bfloat16)
    tok = floats.shape[0]
    top = ids_ref.shape[0]
    named = lax.rem(plane_ref[0] + lax.broadcasted_iota(jnp.int32, (8, tok), 0), experts)
    member = named == ids_ref[0:1, :]
    for k in range(1, top):
        member = member | (named == ids_ref[k : k + 1, :])
    member = jnp.where(member, 1.0, 0.0)
    before = lax.broadcasted_iota(jnp.int32, (tok, tok), 0) < lax.broadcasted_iota(jnp.int32, (tok, tok), 1)
    rank = jnp.dot(
        member.astype(jnp.bfloat16),
        jnp.where(before, 1.0, 0.0).astype(jnp.bfloat16),
        preferred_element_type=jnp.float32,
    )
    slot = lax.broadcasted_iota(jnp.int32, (cap, tok), 0).astype(jnp.float32)
    for d in range(experts):
        pick = jnp.where(slot == rank[d : d + 1, :], member[d : d + 1, :], 0.0).astype(jnp.bfloat16)
        out_refs[d][...] = jnp.dot(pick, normed, preferred_element_type=jnp.float32).astype(jnp.bfloat16)


def dispatch(plane, ids, tokens, gain, bias, cap, experts):
    width = tokens.shape[1]
    vmem = pl.BlockSpec(memory_space=pltpu.VMEM)
    return pl.pallas_call(
        functools.partial(dispatch_kernel, cap, experts),
        out_shape=[pltpu.VMEM((cap, width), jnp.bfloat16)] * experts,
        in_specs=[pl.BlockSpec(memory_space=pltpu.SMEM)] + [vmem] * 4,
        out_specs=[vmem] * experts,
        compiler_params=pltpu.CompilerParams(vmem_limit_bytes=8 << 20),
        name="dispatch",
    )(plane, in_hbm(ids.T), in_hbm(tokens), in_hbm(gain[None, :]), in_hbm(bias[None, :]))


def routing_kernel(cap, experts, plane_ref, ids_ref, gates_ref, tokens_ref, b_out_ref, base_ref, gate_ref, *pick_refs):
    top, tok = ids_ref.shape
    named = lax.rem(plane_ref[0] + lax.broadcasted_iota(jnp.int32, (8, tok), 0), experts)
    member = jnp.zeros((8, tok), jnp.float32)
    gate = jnp.zeros((8, tok), jnp.float32)
    for k in range(top):
        hit = named == ids_ref[k : k + 1, :]
        member = jnp.where(hit, 1.0, member)
        gate = jnp.where(hit, gates_ref[k : k + 1, :], gate)
    row, column = (lax.broadcasted_iota(jnp.int32, (tok, tok), axis) for axis in (0, 1))
    rank = jnp.dot(
        member.astype(jnp.bfloat16),
        jnp.where(row < column, 1.0, 0.0).astype(jnp.bfloat16),
        preferred_element_type=jnp.float32,
    )
    rank = jnp.where(member > 0.0, rank, -1.0)
    turn = jnp.where(row == column, 1.0, 0.0)
    flip = functools.partial(
        lax.dot_general,
        turn,
        dimension_numbers=(((1,), (1,)), ((), ())),
        precision=lax.Precision.HIGHEST,
        preferred_element_type=jnp.float32,
    )
    rank, gate = flip(rank), flip(gate)
    gate_ref[...] = gate
    slot = lax.broadcasted_iota(jnp.int32, (tok, cap), 1).astype(jnp.float32)
    base = tokens_ref[...].astype(jnp.float32)
    for d in range(experts):
        pick_refs[d][...] = jnp.where(slot == rank[:, d : d + 1], 1.0, 0.0).astype(jnp.bfloat16)
        bias = b_out_ref[pl.ds(lax.rem(plane_ref[0] + d, experts), 1), :]
        base += gate[:, d : d + 1] * bias
    base_ref[...] = base


def routing(plane, ids, gates, tokens, b_out, cap):
    experts, tok = b_out.shape[0], tokens.shape[0]
    vmem = pl.BlockSpec(memory_space=pltpu.VMEM)
    return pl.pallas_call(
        functools.partial(routing_kernel, cap, experts),
        out_shape=[pltpu.VMEM(tokens.shape, jnp.float32), pltpu.VMEM((tok, 8), jnp.float32)]
        + [pltpu.VMEM((tok, cap), jnp.bfloat16)] * experts,
        in_specs=[pl.BlockSpec(memory_space=pltpu.SMEM)] + [vmem] * 4,
        out_specs=[vmem] * (2 + experts),
        compiler_params=pltpu.CompilerParams(vmem_limit_bytes=8 << 20),
        name="routing",
    )(plane, in_hbm(ids.T), in_hbm(gates.T), in_hbm(tokens), in_hbm(b_out))


def combine_kernel(base_ref, gate_ref, *refs):
    experts = len(refs) // 2
    total = base_ref[...]
    for d in range(experts):
        rows = jnp.dot(refs[d][...], refs[experts + d][...], preferred_element_type=jnp.float32)
        total += gate_ref[:, d : d + 1] * rows
    refs[-1][...] = total.astype(jnp.bfloat16)


def combine(routed, rows):
    vmem = pl.BlockSpec(memory_space=pltpu.VMEM)
    return pl.pallas_call(
        combine_kernel,
        out_shape=jax.ShapeDtypeStruct(routed[0].shape, jnp.bfloat16),
        in_specs=[vmem] * (len(routed) + len(rows)),
        out_specs=vmem,
        compiler_params=pltpu.CompilerParams(vmem_limit_bytes=8 << 20),
        name="combine",
    )(*[in_vmem(value) for value in (*routed, *rows)])


def stage_kernel(*refs):
    count = len(refs) // 3
    sources, targets, sems = refs[:count], refs[count : 2 * count], refs[2 * count :]
    copies = [pltpu.make_async_copy(*three) for three in zip(sources, targets, sems)]
    for copy in copies:
        copy.start()
    for copy in copies:
        copy.wait()


def stage(*arrays):
    return pl.pallas_call(
        stage_kernel,
        out_shape=[pltpu.VMEM(array.shape, array.dtype) for array in arrays],
        in_specs=[pl.BlockSpec(memory_space=pl.ANY)] * len(arrays),
        out_specs=[pl.BlockSpec(memory_space=pltpu.VMEM)] * len(arrays),
        scratch_shapes=[pltpu.SemaphoreType.DMA] * len(arrays),
        compiler_params=pltpu.CompilerParams(vmem_limit_bytes=4 << 20),
        name="stage",
    )(*[in_hbm(array) for array in arrays])


def feed_forward(count, tile, weights, rows, hidden, put):
    in_0, in_1, bias_0, bias_1, out_0, out_1 = weights
    units, width = out_0.shape
    for k, (w_in, bias) in enumerate(((in_0, bias_0), (in_1, bias_1))):
        for t in range(units // tile):
            cols = slice(t * tile, (t + 1) * tile)
            sums = jnp.dot(rows[...], w_in[:, cols], preferred_element_type=jnp.float32) + bias[:, cols]
            hidden[:, k * units + t * tile : k * units + (t + 1) * tile] = jnp.maximum(sums, 0.0).astype(jnp.bfloat16)
    for t in range(width // tile):
        cols = slice(t * tile, (t + 1) * tile)
        sums = jnp.dot(hidden[:, :units], out_0[:, cols], preferred_element_type=jnp.float32)
        sums += jnp.dot(hidden[:, units:], out_1[:, cols], preferred_element_type=jnp.float32)
        put(t * tile, (t + 1) * tile, sums)


def expert_kernel(tile, *refs):
    pieces = (len(refs) - 8) // 2
    row_refs, weights, sum_refs, (rows, hidden) = refs[:pieces], refs[pieces : pieces + 6], refs[pieces + 6 : -2], refs[-2:]
    count = row_refs[0].shape[0]
    width = rows.shape[1]
    places = []
    start = column = 0
    for ref in row_refs:
        places.append((start, column))
        rows[start : start + count, column : column + ref.shape[1]] = ref[...]
        column = (column + ref.shape[1]) % width
        start += 0 if column else count

    def put(first, last, sums):
        for ref, (start, column) in zip(sum_refs, places):
            if column <= first < column + ref.shape[1]:
                piece = sums[start : start + count, :].astype(ref.dtype)
                ref[:, first - column : last - column] = piece

    feed_forward(count, tile, weights, rows, hidden, put)


def expert_rows(rows, weights, kinds):
    count, width = rows[0].shape[0], weights[0].shape[0]
    units = weights[0].shape[1]
    total = count * sum(value.shape[1] for value in rows) // width
    vmem = pl.BlockSpec(memory_space=pltpu.VMEM)
    return pl.pallas_call(
        functools.partial(expert_kernel, 512),
        out_shape=[pltpu.VMEM(value.shape, kind) for value, kind in zip(rows, kinds)],
        in_specs=[vmem] * (len(rows) + 6),
        out_specs=[vmem] * len(rows),
        scratch_shapes=[pltpu.VMEM((total, width), jnp.bfloat16), pltpu.VMEM((total, 2 * units), jnp.bfloat16)],
        compiler_params=pltpu.CompilerParams(vmem_limit_bytes=16 << 20),
        name="expert",
    )(*[in_vmem(value) for value in (*rows, *weights)])


def local(tokens, expert_ids, gate_weights, norm_gain, norm_bias, w_in, b_in, w_out, b_out):
    tok_dev = tokens.shape[0]
    top_count = expert_ids.shape[1]
    devices = lax.axis_size("local")
    experts = b_out.shape[0]
    shared = devices // experts
    assert shared == 8
    slot_cap = min(
        tok_dev, shared * max(1, (3 * tok_dev * top_count // (2 * experts) + shared - 1) // shared)
    )
    slot_cap += -slot_cap % 16
    plane = (lax.axis_index("local") // shared).reshape(1).astype(jnp.int32)

    def across(value, bit):
        return lax.ppermute(value, "local", [(i, i ^ bit) for i in range(devices)])

    def along(value, planes):
        return lax.ppermute(value, "local", [(i, (i + planes * shared) % devices) for i in range(devices)])

    w_in, w_out = w_in[0], w_out[0]
    half = tokens.shape[1] // 2
    sent = {}

    def put(name, make, *args):
        with jax.named_scope(name):
            sent[name] = make(*args)

    def join(*names, ordered=()):
        for early, late in zip(ordered, ordered[1:]):
            sent[late] = lax.optimization_barrier((sent[late], sent[early]))[0]
        names += ordered
        values = lax.optimization_barrier([sent[name] for name in names])
        sent.update(zip(names, values))

    def fold(sums, low, high):
        to_x = jnp.concatenate([sums[1][:, :half] + low.astype(jnp.float32), sums[1][:, half:]], axis=1)
        to_y = jnp.concatenate([sums[2][:, :half], sums[2][:, half:] + high.astype(jnp.float32)], axis=1)
        return to_x.astype(jnp.bfloat16), to_y.astype(jnp.bfloat16)

    def total(sums, *others):
        return (sums[0] + sum(value.astype(jnp.float32) for value in others)).astype(jnp.bfloat16)

    near = sorted({1, experts - 1})
    far = list(range(2, experts - 1))
    wide, short = jnp.float32, jnp.bfloat16
    blocks = dispatch(plane, expert_ids, tokens, norm_gain, norm_bias, slot_cap, experts)
    own = blocks[0]
    put("w1", across, w_in, 1)
    put("z1", along, blocks[near[0]], near[0])
    put("z3", along, blocks[near[-1]], near[-1])
    put("ox", across, own, 2)
    put("oy", across, own, 4)
    put("od", across, own, 6)
    sent["mine"], sent["own"], sent["plane"] = [w_in, w_out], own, plane
    join("mine", "own", "plane")
    put("K", stage, *sent["mine"])
    put("P", routing, sent["plane"], expert_ids, gate_weights, tokens, b_out, slot_cap)
    sent["out"], sent["bias"], sent["blocks"] = w_out, b_in, [blocks[d] for d in far]
    join("P", "own", "out", "bias", "blocks", ordered=("z1", "z3", "ox", "oy", "w1", "K"))
    mine_in, mine_out = sent["K"]
    near_rows = jnp.concatenate([sent["z1"], sent["z3"]][: len(near)])
    put("w2", across, sent["out"], 1)
    put("A1x", across, near_rows, 2)
    put("A1y", across, near_rows, 4)
    put("z2", lambda: [along(block, d) for block, d in zip(sent["blocks"], far)])
    put("b", across, sent["bias"], 1)
    put("K2", stage, sent["w1"], sent["w2"])
    join("A1x", "A1y", "K2", "b")
    peer_in, peer_out = sent["K2"]
    weights = (mine_in, peer_in, b_in, sent["b"], mine_out, peer_out)
    far_rows = jnp.concatenate(sent["z2"]) if len(far) > 1 else sent["z2"][0]
    put("A2a", across, sent["A1x"][:, :half], 4)
    put("A2b", across, sent["A1y"][:, half:], 2)
    put("B1x", across, far_rows, 2)
    put("B1y", across, far_rows, 4)
    put("bd", across, far_rows, 6)
    put("EA1", expert_rows, [near_rows, sent["A1x"], sent["A1y"]], weights, [wide] * 3)
    join("EA1", "A2a", "A2b", "od")
    put("EA2", expert_rows, [sent["A2a"], sent["A2b"]], weights, [short] * 2)
    join("EA2", "B1x", "B1y")
    put("AR1a", across, sent["EA2"][0], 4)
    put("AR1b", across, sent["EA2"][1], 2)
    rows = [far_rows, *(sent[name] for name in ("B1x", "B1y", "bd"))]
    put("EB", expert_rows, rows, weights, [wide] + [short] * 3)
    join("EB", "AR1a", "AR1b")
    to_x, to_y = fold(sent["EA1"], sent["AR1a"], sent["AR1b"])
    put("AR2x", across, to_x, 2)
    put("AR2y", across, to_y, 4)
    for part, piece, bits in zip("xyd", sent["EB"][1:], (2, 4, 6)):
        put("BR" + part, across, piece, bits)
    rows = [sent["own"], sent["ox"], sent["oy"], sent["od"]]
    rows, sent["EB"] = lax.optimization_barrier((rows, list(sent["EB"])))
    put("EO", expert_rows, rows, weights, [wide] + [short] * 3)
    join("AR2x", "AR2y", "EO")
    value = total(sent["EA1"], sent["AR2x"], sent["AR2y"])
    for i, d in enumerate(near):
        put("c1" if i == 0 else "c3", along, value[i * slot_cap : (i + 1) * slot_cap], -d)
    join("BRx", "BRy", "BRd")
    value = total(sent["EB"], *(sent[name] for name in ("BRx", "BRy", "BRd")))
    put("c2", lambda: [along(value[i * slot_cap : (i + 1) * slot_cap], -d) for i, d in enumerate(far)])
    for part, piece, bits in zip("xyd", sent["EO"][1:], (2, 4, 6)):
        put("OR" + part, across, piece, bits)
    rows = dict(zip(far, sent["c2"]))
    rows[near[0]], rows[near[-1]] = sent["c1"], sent["c3"]
    rows[0] = total(sent["EO"], sent["ORx"], sent["ORy"], sent["ORd"])
    results = [rows[d] for d in range(experts)]
    return combine(sent["P"], results)


def solution(mesh):
    in_specs = (
        P(("groups", "local"), None),
        P(("groups", "local"), None),
        P(("groups", "local"), None),
        P(),
        P(),
        P("local", None, None),
        P("local", None),
        P("local", None, None),
        P(),
    )
    out_specs = P(("groups", "local"), None)
    return jax.shard_map(local, mesh=mesh, in_specs=in_specs, out_specs=out_specs, check_vma=False)
```

```python
import functools

import jax
import jax.numpy as jnp
from jax import lax
from jax.experimental import pallas as pl
from jax.experimental.pallas import tpu as pltpu
from jax.sharding import PartitionSpec as P


def in_vmem(value):
    return pltpu.with_memory_space_constraint(value, pltpu.VMEM)


def in_hbm(value):
    return pltpu.with_memory_space_constraint(value, pltpu.HBM)


def dispatch_kernel(cap, experts, plane_ref, ids_ref, tokens_ref, gain_ref, bias_ref, *out_refs):
    floats = tokens_ref[...].astype(jnp.float32)
    row_mean = jnp.mean(floats, axis=-1, keepdims=True)
    centered = floats - row_mean
    row_var = jnp.mean(centered * centered, axis=-1, keepdims=True)
    normed = centered * lax.rsqrt(row_var + 1e-05) * gain_ref[...] + bias_ref[...]
    normed = normed.astype(jnp.bfloat16)
    tok = floats.shape[0]
    top = ids_ref.shape[0]
    named = lax.rem(plane_ref[0] + lax.broadcasted_iota(jnp.int32, (8, tok), 0), experts)
    member = named == ids_ref[0:1, :]
    for k in range(1, top):
        member = member | (named == ids_ref[k : k + 1, :])
    member = jnp.where(member, 1.0, 0.0)
    before = lax.broadcasted_iota(jnp.int32, (tok, tok), 0) < lax.broadcasted_iota(jnp.int32, (tok, tok), 1)
    rank = jnp.dot(
        member.astype(jnp.bfloat16),
        jnp.where(before, 1.0, 0.0).astype(jnp.bfloat16),
        preferred_element_type=jnp.float32,
    )
    slot = lax.broadcasted_iota(jnp.int32, (cap, tok), 0).astype(jnp.float32)
    for d in range(experts):
        pick = jnp.where(slot == rank[d : d + 1, :], member[d : d + 1, :], 0.0).astype(jnp.bfloat16)
        out_refs[d][...] = jnp.dot(pick, normed, preferred_element_type=jnp.float32).astype(jnp.bfloat16)


def dispatch(plane, ids, tokens, gain, bias, cap, experts):
    width = tokens.shape[1]
    vmem = pl.BlockSpec(memory_space=pltpu.VMEM)
    return pl.pallas_call(
        functools.partial(dispatch_kernel, cap, experts),
        out_shape=[pltpu.VMEM((cap, width), jnp.bfloat16)] * experts,
        in_specs=[pl.BlockSpec(memory_space=pltpu.SMEM)] + [vmem] * 4,
        out_specs=[vmem] * experts,
        compiler_params=pltpu.CompilerParams(vmem_limit_bytes=8 << 20),
        name="dispatch",
    )(plane, in_hbm(ids.T), in_hbm(tokens), in_hbm(gain[None, :]), in_hbm(bias[None, :]))


def routing_kernel(cap, experts, plane_ref, ids_ref, gates_ref, tokens_ref, b_out_ref, base_ref, gate_ref, *pick_refs):
    top, tok = ids_ref.shape
    named = lax.rem(plane_ref[0] + lax.broadcasted_iota(jnp.int32, (8, tok), 0), experts)
    member = jnp.zeros((8, tok), jnp.float32)
    gate = jnp.zeros((8, tok), jnp.float32)
    for k in range(top):
        hit = named == ids_ref[k : k + 1, :]
        member = jnp.where(hit, 1.0, member)
        gate = jnp.where(hit, gates_ref[k : k + 1, :], gate)
    row, column = (lax.broadcasted_iota(jnp.int32, (tok, tok), axis) for axis in (0, 1))
    rank = jnp.dot(
        member.astype(jnp.bfloat16),
        jnp.where(row < column, 1.0, 0.0).astype(jnp.bfloat16),
        preferred_element_type=jnp.float32,
    )
    rank = jnp.where(member > 0.0, rank, -1.0)
    turn = jnp.where(row == column, 1.0, 0.0)
    flip = functools.partial(
        lax.dot_general,
        turn,
        dimension_numbers=(((1,), (1,)), ((), ())),
        precision=lax.Precision.HIGHEST,
        preferred_element_type=jnp.float32,
    )
    rank, gate = flip(rank), flip(gate)
    gate_ref[...] = gate
    slot = lax.broadcasted_iota(jnp.int32, (tok, cap), 1).astype(jnp.float32)
    base = tokens_ref[...].astype(jnp.float32)
    for d in range(experts):
        pick_refs[d][...] = jnp.where(slot == rank[:, d : d + 1], 1.0, 0.0).astype(jnp.bfloat16)
        bias = b_out_ref[pl.ds(lax.rem(plane_ref[0] + d, experts), 1), :]
        base += gate[:, d : d + 1] * bias
    base_ref[...] = base


def routing(plane, ids, gates, tokens, b_out, cap):
    experts, tok = b_out.shape[0], tokens.shape[0]
    vmem = pl.BlockSpec(memory_space=pltpu.VMEM)
    return pl.pallas_call(
        functools.partial(routing_kernel, cap, experts),
        out_shape=[pltpu.VMEM(tokens.shape, jnp.float32), pltpu.VMEM((tok, 8), jnp.float32)]
        + [pltpu.VMEM((tok, cap), jnp.bfloat16)] * experts,
        in_specs=[pl.BlockSpec(memory_space=pltpu.SMEM)] + [vmem] * 4,
        out_specs=[vmem] * (2 + experts),
        compiler_params=pltpu.CompilerParams(vmem_limit_bytes=8 << 20),
        name="routing",
    )(plane, in_hbm(ids.T), in_hbm(gates.T), in_hbm(tokens), in_hbm(b_out))


def combine_kernel(base_ref, gate_ref, *refs):
    experts = len(refs) // 2
    total = base_ref[...]
    for d in range(experts):
        rows = jnp.dot(refs[d][...], refs[experts + d][...], preferred_element_type=jnp.float32)
        total += gate_ref[:, d : d + 1] * rows
    refs[-1][...] = total.astype(jnp.bfloat16)


def combine(routed, rows):
    vmem = pl.BlockSpec(memory_space=pltpu.VMEM)
    return pl.pallas_call(
        combine_kernel,
        out_shape=jax.ShapeDtypeStruct(routed[0].shape, jnp.bfloat16),
        in_specs=[vmem] * (len(routed) + len(rows)),
        out_specs=vmem,
        compiler_params=pltpu.CompilerParams(vmem_limit_bytes=8 << 20),
        name="combine",
    )(*[in_vmem(value) for value in (*routed, *rows)])


def stage_kernel(*refs):
    count = len(refs) // 3
    sources, targets, sems = refs[:count], refs[count : 2 * count], refs[2 * count :]
    copies = [pltpu.make_async_copy(*three) for three in zip(sources, targets, sems)]
    for copy in copies:
        copy.start()
    for copy in copies:
        copy.wait()


def stage(*arrays):
    return pl.pallas_call(
        stage_kernel,
        out_shape=[pltpu.VMEM(array.shape, array.dtype) for array in arrays],
        in_specs=[pl.BlockSpec(memory_space=pl.ANY)] * len(arrays),
        out_specs=[pl.BlockSpec(memory_space=pltpu.VMEM)] * len(arrays),
        scratch_shapes=[pltpu.SemaphoreType.DMA] * len(arrays),
        compiler_params=pltpu.CompilerParams(vmem_limit_bytes=4 << 20),
        name="stage",
    )(*[in_hbm(array) for array in arrays])


def feed_forward(count, tile, weights, rows, hidden, put):
    in_0, in_1, bias_0, bias_1, out_0, out_1 = weights
    units, width = out_0.shape
    for k, (w_in, bias) in enumerate(((in_0, bias_0), (in_1, bias_1))):
        for t in range(units // tile):
            cols = slice(t * tile, (t + 1) * tile)
            sums = jnp.dot(rows[...], w_in[:, cols], preferred_element_type=jnp.float32) + bias[:, cols]
            hidden[:, k * units + t * tile : k * units + (t + 1) * tile] = jnp.maximum(sums, 0.0).astype(jnp.bfloat16)
    for t in range(width // tile):
        cols = slice(t * tile, (t + 1) * tile)
        sums = jnp.dot(hidden[:, :units], out_0[:, cols], preferred_element_type=jnp.float32)
        sums += jnp.dot(hidden[:, units:], out_1[:, cols], preferred_element_type=jnp.float32)
        put(t * tile, (t + 1) * tile, sums)


def expert_kernel(tile, *refs):
    pieces = (len(refs) - 8) // 2
    row_refs, weights, sum_refs, (rows, hidden) = refs[:pieces], refs[pieces : pieces + 6], refs[pieces + 6 : -2], refs[-2:]
    count = row_refs[0].shape[0]
    width = rows.shape[1]
    places = []
    start = column = 0
    for ref in row_refs:
        places.append((start, column))
        rows[start : start + count, column : column + ref.shape[1]] = ref[...]
        column = (column + ref.shape[1]) % width
        start += 0 if column else count

    def put(first, last, sums):
        for ref, (start, column) in zip(sum_refs, places):
            if column <= first < column + ref.shape[1]:
                piece = sums[start : start + count, :].astype(ref.dtype)
                ref[:, first - column : last - column] = piece

    feed_forward(count, tile, weights, rows, hidden, put)


def expert_rows(rows, weights, kinds):
    count, width = rows[0].shape[0], weights[0].shape[0]
    units = weights[0].shape[1]
    total = count * sum(value.shape[1] for value in rows) // width
    vmem = pl.BlockSpec(memory_space=pltpu.VMEM)
    return pl.pallas_call(
        functools.partial(expert_kernel, 512),
        out_shape=[pltpu.VMEM(value.shape, kind) for value, kind in zip(rows, kinds)],
        in_specs=[vmem] * (len(rows) + 6),
        out_specs=[vmem] * len(rows),
        scratch_shapes=[pltpu.VMEM((total, width), jnp.bfloat16), pltpu.VMEM((total, 2 * units), jnp.bfloat16)],
        compiler_params=pltpu.CompilerParams(vmem_limit_bytes=16 << 20),
        name="expert",
    )(*[in_vmem(value) for value in (*rows, *weights)])


def local(tokens, expert_ids, gate_weights, norm_gain, norm_bias, w_in, b_in, w_out, b_out):
    tok_dev = tokens.shape[0]
    top_count = expert_ids.shape[1]
    devices = lax.axis_size("local")
    experts = b_out.shape[0]
    shared = devices // experts
    assert shared == 8
    slot_cap = min(
        tok_dev, shared * max(1, (3 * tok_dev * top_count // (2 * experts) + shared - 1) // shared)
    )
    slot_cap += -slot_cap % 16
    plane = (lax.axis_index("local") // shared).reshape(1).astype(jnp.int32)

    def across(value, bit):
        return lax.ppermute(value, "local", [(i, i ^ bit) for i in range(devices)])

    def along(value, planes):
        return lax.ppermute(value, "local", [(i, (i + planes * shared) % devices) for i in range(devices)])

    w_in, w_out = w_in[0], w_out[0]
    half = tokens.shape[1] // 2
    sent = {}

    def put(name, make, *args):
        with jax.named_scope(name):
            sent[name] = make(*args)

    def join(*names, ordered=()):
        for early, late in zip(ordered, ordered[1:]):
            sent[late] = lax.optimization_barrier((sent[late], sent[early]))[0]
        names += ordered
        values = lax.optimization_barrier([sent[name] for name in names])
        sent.update(zip(names, values))

    def fold(sums, low, high):
        to_x = jnp.concatenate([sums[1][:, :half] + low.astype(jnp.float32), sums[1][:, half:]], axis=1)
        to_y = jnp.concatenate([sums[2][:, :half], sums[2][:, half:] + high.astype(jnp.float32)], axis=1)
        return to_x.astype(jnp.bfloat16), to_y.astype(jnp.bfloat16)

    def total(sums, *others):
        return (sums[0] + sum(value.astype(jnp.float32) for value in others)).astype(jnp.bfloat16)

    near = sorted({1, experts - 1})
    far = list(range(2, experts - 1))
    wide, short = jnp.float32, jnp.bfloat16
    blocks = dispatch(plane, expert_ids, tokens, norm_gain, norm_bias, slot_cap, experts)
    own = blocks[0]
    put("w1", across, w_in, 1)
    put("z1", along, blocks[near[0]], near[0])
    put("z3", along, blocks[near[-1]], near[-1])
    put("ox", across, own, 2)
    put("oy", across, own, 4)
    put("od", across, own, 6)
    sent["mine"], sent["own"], sent["plane"] = [w_in, w_out], own, plane
    join("mine", "own", "plane")
    put("K", stage, *sent["mine"])
    put("P", routing, sent["plane"], expert_ids, gate_weights, tokens, b_out, slot_cap)
    sent["out"], sent["bias"], sent["blocks"] = w_out, b_in, [blocks[d] for d in far]
    join("P", "own", "out", "bias", "blocks", ordered=("z1", "z3", "ox", "oy", "w1", "K"))
    mine_in, mine_out = sent["K"]
    near_rows = jnp.concatenate([sent["z1"], sent["z3"]][: len(near)])
    put("w2", across, sent["out"], 1)
    put("A1x", across, near_rows, 2)
    put("A1y", across, near_rows, 4)
    put("z2", lambda: [along(block, d) for block, d in zip(sent["blocks"], far)])
    put("b", across, sent["bias"], 1)
    put("K2", stage, sent["w1"])
    join("A1x", "A1y", "K2", "b")
    (peer_in,), peer_out = sent["K2"], sent["w2"]
    weights = (mine_in, peer_in, b_in, sent["b"], mine_out, peer_out)
    far_rows = jnp.concatenate(sent["z2"]) if len(far) > 1 else sent["z2"][0]
    put("A2a", across, sent["A1x"][:, :half], 4)
    put("A2b", across, sent["A1y"][:, half:], 2)
    put("B1x", across, far_rows, 2)
    put("B1y", across, far_rows, 4)
    put("bd", across, far_rows, 6)
    put("EA1", expert_rows, [near_rows, sent["A1x"], sent["A1y"]], weights, [wide] * 3)
    join("EA1", "A2a", "A2b", "od")
    put("EA2", expert_rows, [sent["A2a"], sent["A2b"]], weights, [short] * 2)
    join("EA2", "B1x", "B1y")
    put("AR1a", across, sent["EA2"][0], 4)
    put("AR1b", across, sent["EA2"][1], 2)
    rows = [far_rows, *(sent[name] for name in ("B1x", "B1y", "bd"))]
    put("EB", expert_rows, rows, weights, [wide] + [short] * 3)
    join("EB", "AR1a", "AR1b")
    to_x, to_y = fold(sent["EA1"], sent["AR1a"], sent["AR1b"])
    put("AR2x", across, to_x, 2)
    put("AR2y", across, to_y, 4)
    for part, piece, bits in zip("xyd", sent["EB"][1:], (2, 4, 6)):
        put("BR" + part, across, piece, bits)
    rows = [sent["own"], sent["ox"], sent["oy"], sent["od"]]
    rows, sent["EB"] = lax.optimization_barrier((rows, list(sent["EB"])))
    put("EO", expert_rows, rows, weights, [wide] + [short] * 3)
    join("AR2x", "AR2y", "EO")
    value = total(sent["EA1"], sent["AR2x"], sent["AR2y"])
    for i, d in enumerate(near):
        put("c1" if i == 0 else "c3", along, value[i * slot_cap : (i + 1) * slot_cap], -d)
    join("BRx", "BRy", "BRd")
    value = total(sent["EB"], *(sent[name] for name in ("BRx", "BRy", "BRd")))
    put("c2", lambda: [along(value[i * slot_cap : (i + 1) * slot_cap], -d) for i, d in enumerate(far)])
    for part, piece, bits in zip("xyd", sent["EO"][1:], (2, 4, 6)):
        put("OR" + part, across, piece, bits)
    rows = dict(zip(far, sent["c2"]))
    rows[near[0]], rows[near[-1]] = sent["c1"], sent["c3"]
    rows[0] = total(sent["EO"], sent["ORx"], sent["ORy"], sent["ORd"])
    results = [rows[d] for d in range(experts)]
    return combine(sent["P"], results)


def solution(mesh):
    in_specs = (
        P(("groups", "local"), None),
        P(("groups", "local"), None),
        P(("groups", "local"), None),
        P(),
        P(),
        P("local", None, None),
        P("local", None),
        P("local", None, None),
        P(),
    )
    out_specs = P(("groups", "local"), None)
    return jax.shard_map(local, mesh=mesh, in_specs=in_specs, out_specs=out_specs, check_vma=False)
```
